128 devices in a mesh: dp: 8 (over y, core), fsdp: 16 (over z, x).
Axes of the slice: x: 4, y: 4, z: 4, core: 2. Of those that a mesh axis runs over, the one named last changes fastest.
Arguments:
- old_shards: bfloat16 [8, 16, 38230, 128], P('dp', 'fsdp'), may hold values from -0.0625 to 0.0625
- shard_table: int32 [96, 4], replicated, may hold values from 0 to 917501, as said below
- tokens: bfloat16 [2048, 8192], P('dp', 'fsdp'), may hold values from -6 to 6
- cotangent: bfloat16 [2048, 14336], P('fsdp', 'dp'), may hold values from -0.125 to 0.125
Outputs:
- grad_gate: bfloat16 [8192, 14336], P('fsdp', 'dp')
- grad_up: bfloat16 [8192, 14336], P('fsdp', 'dp')
The draws below stay inside these ranges and needn't reach their ends.
Inputs may be any that keep to these rules, and one draw needn't show every extreme that they name: `shard_table`: rows run over matrix m, then row block f of 57344 128-value rows, then j < 3; shard (m, f, j) begins within block f, is held by device (dp m * 3 + j, fsdp f), and ends where the next shard of its matrix begins (the last at 917504); the first shard of each matrix begins at 0, and the last shard of the up projection begins at 8192 * 112 - 57344 % 3 - 1. Lengths run from 1 to 38229, and that largest length is reached in every draw.
All inputs are finite; a program needn't handle non-finite values.
Results may differ from the reference program's by a relative error of at most 0.023.
Values may be sent and summed in bfloat16 or wider, within the bound.
No kernel may reach another device: no remote copies, remote signals or barrier semaphores. Data moves between devices by JAX's collectives and lax.ppermute only.
A program may use at most 192 MiB of HBM per device.

```python
import jax
import jax.numpy as jnp
from jax import lax

D = 8192
FF = 14336
TOKENS = 2048
DF = 512
QN = 112
KB = 3
OLD_SHARDS = 96
BLOCK_UNITS = 57344
SPACING = 19114
OLD_CAP = 38230
N_DP = 8
N_FSDP = 16


def draw_shard_table(key, part):
    key = jax.random.fold_in(key, 7)
    index = jnp.arange(OLD_SHARDS, dtype=jnp.int32)
    matrix_id = index // (N_FSDP * KB)
    block_id = index // KB % N_FSDP
    within = index % KB
    jitter = jax.random.randint(key, (OLD_SHARDS,), 0, SPACING, dtype=jnp.int32)
    jitter = jnp.where((block_id == 0) & (within == 0), 0, jitter)
    jitter = jnp.where((matrix_id == 0) & (block_id == 0) & (within == KB - 1), 0, jitter)
    jitter = jnp.where((matrix_id == 0) & (block_id == 1) & (within == 0), SPACING - 1, jitter)
    jitter = jnp.where((matrix_id == 1) & (block_id == N_FSDP - 1) & (within == KB - 1), SPACING - 1, jitter)
    first_unit = block_id * BLOCK_UNITS + within * SPACING + jitter
    following = jnp.concatenate([first_unit[1:], jnp.zeros((1,), jnp.int32)])
    closing = (block_id == N_FSDP - 1) & (within == KB - 1)
    following = jnp.where(closing, D * QN, following)
    unit_count = following - first_unit
    holder_dp = matrix_id * KB + within
    return jnp.stack([first_unit, unit_count, holder_dp, block_id], axis=1).astype(jnp.int32)


def shard_levels(key, shape, cuts, smallest, high):
    gain, own = 1.0, jax.random.fold_in(key, 6)
    for axis_at, shards_of in cuts:
        heights = jnp.exp(jax.random.uniform(jax.random.fold_in(own, axis_at), (shards_of,), jnp.float32, smallest / len(cuts), high / len(cuts)))
        gain = gain * jnp.repeat(heights, shape[axis_at] // shards_of).reshape([-1 if axis == axis_at else 1 for axis in range(len(shape))])
    return gain


def scatter_about(key, extent, deviation, limit, cuts=(), held_as=jnp.bfloat16):
    result = deviation * jax.random.normal(key, extent, jnp.float32)
    if cuts:
        result = result * shard_levels(key, extent, cuts, -0.22, 0.18)
    return jnp.clip(result, -limit, limit).astype(held_as)


def setup_inputs(seed: int = 0) -> dict:
    splits = jax.random.split(jax.random.key(seed), 5)
    return {
        "old_shards": scatter_about(splits[0], (N_DP, N_FSDP, OLD_CAP, 128), D ** -0.5, 0.0625, ((0, 8), (1, 16))),
        "shard_table": draw_shard_table(jax.random.fold_in(splits[4], 71), 0),
        "tokens": scatter_about(splits[2], (TOKENS, D), 1.0, 6.0, ((0, 8), (1, 16))),
        "cotangent": scatter_about(splits[3], (TOKENS, FF), TOKENS ** -0.5, 0.125, ((0, 16), (1, 8))),
    }


def relaid_weights(old_shards, shard_table):
    span = D * QN
    flat = jnp.zeros((2 * span + OLD_CAP, 128), jnp.bfloat16)
    positions = jnp.arange(OLD_CAP, dtype=jnp.int32)

    def place(index, flat):
        entry = shard_table[index]
        matrix_id = (index // (N_FSDP * KB)).astype(jnp.int32)
        data = old_shards[entry[2], entry[3]]
        data = jnp.where((positions < entry[1])[:, None], data, jnp.zeros((), jnp.bfloat16))
        where_to = (matrix_id * span + entry[0]).astype(jnp.int32)
        return lax.dynamic_update_slice(flat, data, (where_to, jnp.int32(0)))

    flat = lax.fori_loop(0, OLD_SHARDS, place, flat)
    return flat[:2 * span].reshape(2, D, FF)


def swiglu_backward(summed, upstream):
    gate = summed[:, :FF]
    upper = summed[:, FF:]
    incoming = upstream.astype(jnp.float32)
    sigma = jax.nn.sigmoid(gate)
    grad_gate = incoming * upper * sigma * (1.0 + gate * (1.0 - sigma))
    grad_upper = incoming * gate * sigma
    return jnp.concatenate([grad_gate, grad_upper], axis=1).astype(jnp.bfloat16)


def reference(old_shards, shard_table, tokens, cotangent):
    weights = relaid_weights(old_shards, shard_table)
    joined = jnp.concatenate([weights[0], weights[1]], axis=1)

    def add_block(running, block_index):
        first_feature = (block_index * DF).astype(jnp.int32)
        token_block = lax.dynamic_slice_in_dim(tokens, first_feature, DF, 1)
        weight_block = lax.dynamic_slice_in_dim(joined, first_feature, DF, 0)
        partial_term = jnp.dot(token_block, weight_block, preferred_element_type=jnp.float32).astype(jnp.bfloat16)
        partial_term = lax.optimization_barrier(partial_term)
        return running + partial_term.astype(jnp.float32), None

    summed, _ = lax.scan(add_block, jnp.zeros((TOKENS, 2 * FF), jnp.float32), jnp.arange(N_FSDP, dtype=jnp.int32))
    grads_in = swiglu_backward(summed, cotangent)
    total = lax.dot_general(tokens, grads_in, (((0,), (0,)), ((), ())), preferred_element_type=jnp.float32)
    return total[:, :FF].astype(jnp.bfloat16), total[:, FF:].astype(jnp.bfloat16)
```

```python
import functools

import jax
import jax.numpy as jnp
from jax import lax
from jax.experimental import pallas as pl
from jax.experimental.pallas import tpu as pltpu
from jax.sharding import PartitionSpec as P

LANES = 128
GROUP = 16
ALIGN = 8


def from_ahead(value, axis, steps):
    count = lax.axis_size(axis)
    return lax.ppermute(value, axis, [(source, source - steps) for source in range(steps, count)])


def pack_kernel(place_ref, shard_ref, out_ref, units, *, row_units):
    group = pl.program_id(0)
    lead = place_ref[0]
    length = place_ref[1]
    block = GROUP * row_units
    held = ALIGN * row_units
    n_owner, _, width = out_ref.shape
    owned = width // LANES

    @pl.when(group == 0)
    def _():
        units[:held] = jnp.zeros((held, LANES), jnp.float32)

    @pl.when(group > 0)
    def _():
        units[:held] = units[block : block + held]

    position = group * block + lax.broadcasted_iota(jnp.int32, (block, LANES), 0)
    fresh = shard_ref[...].astype(jnp.float32)
    units[held:] = jnp.where(position < length, fresh, 0.0)
    for column in range(row_units):
        owner, unit = divmod(column, owned)
        rows = units[pl.ds(held - lead + column, GROUP, stride=row_units), :]
        out_ref[owner, :, unit * LANES : (unit + 1) * LANES] = rows.astype(out_ref.dtype)


def pack(place, shard, n_owner, row_units, slab_rows):
    block = GROUP * row_units
    last = pl.cdiv(shard.shape[0], block) - 1
    width = row_units // n_owner * LANES
    return pl.pallas_call(
        functools.partial(pack_kernel, row_units=row_units),
        out_shape=jax.ShapeDtypeStruct((n_owner, slab_rows, width), shard.dtype),
        grid_spec=pltpu.PrefetchScalarGridSpec(
            num_scalar_prefetch=1,
            grid=(slab_rows // GROUP,),
            in_specs=[pl.BlockSpec((block, LANES), lambda g, _: (jnp.minimum(g, last), 0))],
            out_specs=pl.BlockSpec((n_owner, GROUP, width), lambda g, _: (0, g, 0)),
            scratch_shapes=[pltpu.VMEM((block + ALIGN * row_units, LANES), jnp.float32)],
        ),
        compiler_params=pltpu.CompilerParams(vmem_limit_bytes=32 * 1024 * 1024),
        cost_estimate=pl.CostEstimate(
            flops=0, bytes_accessed=4 * shard.size, transcendentals=0
        ),
    )(place, shard)


def unpack_kernel(offset_ref, slab_ref, out_ref, total, *, per_matrix):
    matrix = pl.program_id(0)
    slab_rows = slab_ref.shape[1]
    total[...] = jnp.zeros_like(total)
    for source in range(per_matrix):
        start = pl.multiple_of(offset_ref[matrix * per_matrix + source], ALIGN)
        rows = pl.ds(start, slab_rows)
        total[rows, :] += slab_ref[source].astype(jnp.float32)
    out_ref[...] = total[...].astype(out_ref.dtype)


def unpack(offsets, slabs, per_matrix, rows_out, chunk):
    _, slab_rows, width = slabs.shape
    chunks = width // chunk
    return pl.pallas_call(
        functools.partial(unpack_kernel, per_matrix=per_matrix),
        out_shape=jax.ShapeDtypeStruct((rows_out, 2 * width), slabs.dtype),
        grid_spec=pltpu.PrefetchScalarGridSpec(
            num_scalar_prefetch=1,
            grid=(2, chunks),
            in_specs=[pl.BlockSpec((per_matrix, slab_rows, chunk), lambda m, c, _: (m, 0, c))],
            out_specs=pl.BlockSpec((rows_out, chunk), lambda m, c, _: (0, m * chunks + c)),
            scratch_shapes=[pltpu.VMEM((rows_out, chunk), jnp.float32)],
        ),
        compiler_params=pltpu.CompilerParams(vmem_limit_bytes=32 * 1024 * 1024),
        cost_estimate=pl.CostEstimate(
            flops=0, bytes_accessed=4 * rows_out * width + 2 * slabs.size, transcendentals=0
        ),
    )(offsets, slabs)


def swiglu_backward(summed, upstream, hidden):
    gate = summed[:, :hidden]
    upper = summed[:, hidden:]
    incoming = upstream.astype(jnp.float32)
    sigma = jax.nn.sigmoid(gate)
    grad_gate = incoming * upper * sigma * (1.0 + gate * (1.0 - sigma))
    grad_upper = incoming * gate * sigma
    return jnp.concatenate([grad_gate, grad_upper], axis=1).astype(jnp.bfloat16)


def on_device(old_shards, shard_table, tokens, cotangent):
    n_data = lax.axis_size("dp")
    n_feature = lax.axis_size("fsdp")
    data_index = lax.axis_index("dp")
    feature_index = lax.axis_index("fsdp")
    block_rows = tokens.shape[1]
    hidden = cotangent.shape[1]
    row_units = hidden // LANES * n_data
    capacity = old_shards.shape[2]
    per_block = 3
    first_row = feature_index * block_rows
    slab_rows = pl.cdiv(ALIGN * row_units + capacity, GROUP * row_units) * GROUP
    extended_rows = block_rows + pl.cdiv(slab_rows, LANES) * LANES

    matrix_id = data_index // per_block
    holder = data_index < 2 * per_block
    table_row = (matrix_id * n_feature + feature_index) * per_block + data_index % per_block
    my_entry = lax.dynamic_index_in_dim(
        shard_table, jnp.minimum(table_row, shard_table.shape[0] - 1), 0, keepdims=False
    )
    lead = (my_entry[0] - first_row * row_units) % (ALIGN * row_units)
    place = jnp.stack([lead, jnp.where(holder, my_entry[1], 0)])
    outgoing = pack(place, old_shards[0, 0], n_data, row_units, slab_rows)
    incoming = lax.all_to_all(outgoing, "dp", split_axis=0, concat_axis=0, tiled=True)

    ahead = from_ahead(tokens[:, : extended_rows - block_rows], "fsdp", 1)
    widened = jnp.concatenate([tokens, ahead], axis=1)
    all_rows = lax.all_gather(widened, "dp", axis=0, tiled=True)

    firsts = shard_table[:, 0].reshape(2, n_feature, per_block)
    firsts = lax.dynamic_index_in_dim(firsts, feature_index, 1, keepdims=False).reshape(-1)
    offsets = (firsts // row_units - first_row) // ALIGN * ALIGN
    joined = unpack(offsets, incoming, per_block, extended_rows, 2 * LANES)

    partial_term = jnp.dot(all_rows, joined, preferred_element_type=jnp.float32)
    summed = lax.psum_scatter(
        partial_term.astype(jnp.bfloat16), "fsdp", scatter_dimension=0, tiled=True
    ).astype(jnp.float32)
    grads_own = swiglu_backward(summed, cotangent, hidden)
    grads_in = lax.all_gather(grads_own, "fsdp", axis=0, tiled=True)
    total = lax.dot_general(
        all_rows[:, :block_rows],
        grads_in,
        (((0,), (0,)), ((), ())),
        preferred_element_type=jnp.float32,
    )
    return (total[:, :hidden].astype(jnp.bfloat16), total[:, hidden:].astype(jnp.bfloat16))


def solution(mesh):
    return jax.shard_map(
        on_device,
        mesh=mesh,
        in_specs=(P("dp", "fsdp", None, None), P(), P("dp", "fsdp"), P("fsdp", "dp")),
        out_specs=(P("fsdp", "dp"), P("fsdp", "dp")),
        check_vma=False,
    )
```

```python
import functools

import jax
import jax.numpy as jnp
from jax import lax
from jax.experimental import pallas as pl
from jax.experimental.pallas import tpu as pltpu
from jax.sharding import PartitionSpec as P

LANES = 128
GROUP = 32
ALIGN = 8
SIDE = 4
PER_MATRIX = 3
CHUNKS = ((4, 2), (4, 4))
ORDER = "u0 f0 u1 s0 f1 b0 s1 b1".split()
BRIEF = pl.CostEstimate(flops=1, bytes_accessed=1, transcendentals=0)
VMEM = pltpu.CompilerParams(vmem_limit_bytes=60 * 1024 * 1024)


def full(shape):
    return pl.BlockSpec(shape, lambda *_: (0,) * len(shape))


def low_half(shape):
    return lax.broadcasted_iota(jnp.int32, shape, len(shape) - 1) < LANES // 2


def segments(chunk):
    found, unit, lane = [], 0, 0
    for count in chunk:
        found.append((count, unit, lane))
        unit += count
        lane += 2 * LANES * count // SIDE
    return found


def piece_width(chunk):
    return 2 * LANES * sum(chunk) // SIDE


def swap_halves(value):
    return pltpu.roll(value, LANES // 2, value.ndim - 1)


def pack_kernel(place_ref, shard_ref, *refs, row_units, base):
    out_refs, units = refs[:-1], refs[-1]
    group = pl.program_id(0)
    lead = place_ref[0]
    length = place_ref[1]
    block = GROUP * row_units
    held = ALIGN * row_units
    n_owner = out_refs[0].shape[0]
    owned = row_units // n_owner

    @pl.when(group == 0)
    def _():
        units[:held] = jnp.zeros((held, LANES), jnp.float32)

    @pl.when(group > 0)
    def _():
        units[:held] = units[block : block + held]

    whole = (group + 1) * block <= length

    @pl.when(whole)
    def _():
        units[held:] = shard_ref[...].astype(jnp.float32)

    @pl.when(jnp.logical_not(whole))
    def _():
        position = group * block + lax.broadcasted_iota(jnp.int32, (block, LANES), 0)
        units[held:] = jnp.where(position < length, shard_ref[...].astype(jnp.float32), 0.0)

    for owner in range(n_owner):
        column = owner * owned + base
        for out_ref in out_refs:
            for unit in range(out_ref.shape[2] // LANES):
                rows = units[pl.ds(held - lead + column, GROUP, stride=row_units), :]
                out_ref[owner, :, unit * LANES : (unit + 1) * LANES] = rows.astype(out_ref.dtype)
                column += 1


def pack(place, shard, n_owner, row_units, slab_rows, base, chunks):
    block = GROUP * row_units
    last = pl.cdiv(shard.shape[0], block) - 1
    return pl.pallas_call(
        functools.partial(pack_kernel, row_units=row_units, base=base),
        out_shape=[
            jax.ShapeDtypeStruct((n_owner, slab_rows, sum(n) * LANES), shard.dtype) for n in chunks
        ],
        grid_spec=pltpu.PrefetchScalarGridSpec(
            num_scalar_prefetch=1,
            grid=(slab_rows // GROUP,),
            in_specs=[pl.BlockSpec((block, LANES), lambda g, _: (jnp.minimum(g, last), 0))],
            out_specs=[
                pl.BlockSpec((n_owner, GROUP, sum(n) * LANES), lambda g, _: (0, g, 0)) for n in chunks
            ],
            scratch_shapes=[pltpu.VMEM((block + ALIGN * row_units, LANES), jnp.float32)],
        ),
        compiler_params=VMEM,
        cost_estimate=BRIEF,
    )(place, shard)


def unpack_kernel(meta_ref, slab_ref, *refs, chunk):
    out_refs, total = refs[:SIDE], refs[SIDE]
    slab_rows = slab_ref.shape[1]
    side = meta_ref[2 * PER_MATRIX]

    def gathered(matrix, tile):
        total[...] = jnp.zeros_like(total)
        for source in range(matrix * PER_MATRIX, (matrix + 1) * PER_MATRIX):
            rows = pl.ds(pl.multiple_of(meta_ref[source], ALIGN), slab_rows)
            lanes = pl.ds(pl.multiple_of(tile * LANES, LANES), LANES)
            total[rows, :] += slab_ref[source, :, lanes].astype(jnp.float32)
        return total[...]

    for step, out_ref in enumerate(out_refs):
        part = lax.rem(side + step, SIDE)
        for count, unit, lane in segments(chunk):
            if count == SIDE:
                for matrix in range(2):
                    lanes = slice(lane + matrix * LANES, lane + (matrix + 1) * LANES)
                    out_ref[:, lanes] = gathered(matrix, unit + part).astype(out_ref.dtype)
            else:
                first = lax.rem(part, 2) == 0
                gate = gathered(0, unit + part // 2)
                gate = jnp.where(first, gate, swap_halves(gate))
                upper = gathered(1, unit + part // 2)
                upper = jnp.where(first, swap_halves(upper), upper)
                value = jnp.where(low_half(gate.shape), gate, upper)
                out_ref[:, lane : lane + LANES] = value.astype(out_ref.dtype)


def unpack(meta, slabs, rows_out, chunk):
    _, slab_rows, width = slabs.shape
    out_width = piece_width(chunk)
    sources = 2 * PER_MATRIX
    return pl.pallas_call(
        functools.partial(unpack_kernel, chunk=chunk),
        out_shape=[jax.ShapeDtypeStruct((rows_out, out_width), slabs.dtype)] * SIDE,
        grid_spec=pltpu.PrefetchScalarGridSpec(
            num_scalar_prefetch=1,
            grid=(1,),
            in_specs=[full((sources, slab_rows, width))],
            out_specs=[full((rows_out, out_width))] * SIDE,
            scratch_shapes=[pltpu.VMEM((rows_out, LANES), jnp.float32)],
        ),
        compiler_params=VMEM,
        cost_estimate=BRIEF,
    )(meta, slabs)


def forward_kernel(meta_ref, *refs):
    own, sibling = refs[:SIDE], refs[SIDE : 2 * SIDE]
    edges = refs[2 * SIDE : 2 * SIDE + 2]
    weights = refs[2 * SIDE + 2 : 3 * SIDE + 2]
    out_refs = refs[3 * SIDE + 2 : 4 * SIDE + 2]
    joined = refs[4 * SIDE + 2]
    piece = pl.program_id(0)
    last = meta_ref[SIDE]
    features = own[0].shape[2]
    spill = edges[0].shape[2]
    rows = own[0].shape[1]

    @pl.when(piece == 0)
    def _():
        beyond = None
        for step, weight in enumerate(weights):
            source = (step + 1) % SIDE
            tail = weights[source][features:].astype(jnp.float32)
            inside = jnp.where(last == source, 0.0, tail)
            outside = tail - inside
            beyond = outside if beyond is None else beyond + outside
            head = weight[:spill].astype(jnp.float32) + inside
            first = step * features
            joined[first : first + spill] = head.astype(joined.dtype)
            joined[first + spill : first + features] = weight[spill:features]
        joined[SIDE * features :] = beyond.astype(joined.dtype)

    for half, (parts, edge) in enumerate(((own, edges[0]), (sibling, edges[1]))):
        left = jnp.concatenate([part[0] for part in parts] + [edge[0]], axis=1)
        value = jnp.dot(left, joined[...], preferred_element_type=jnp.float32)
        value = value.astype(jnp.bfloat16)
        for index, out_ref in enumerate(out_refs):

            @pl.when(piece == index)
            def _():
                out_ref[half * rows : (half + 1) * rows] = value


def forward(meta, tokens, edges, weights):
    _, rows, features = tokens[0].shape
    spill = edges.shape[2]
    width = weights[0].shape[1]
    depth = SIDE * features + spill
    block = pl.BlockSpec((1, rows, features), lambda p, m: (m[p], 0, 0))
    edge = lambda first: pl.BlockSpec((1, rows, spill), lambda p, m: (m[first + p], 0, 0))
    return pl.pallas_call(
        forward_kernel,
        out_shape=[jax.ShapeDtypeStruct((2 * rows, width), jnp.bfloat16)] * SIDE,
        grid_spec=pltpu.PrefetchScalarGridSpec(
            num_scalar_prefetch=1,
            grid=(SIDE,),
            in_specs=[block] * (2 * SIDE)
            + [edge(SIDE + 1), edge(2 * SIDE + 1)]
            + [full(weights[0].shape)] * SIDE,
            out_specs=[full((2 * rows, width))] * SIDE,
            scratch_shapes=[pltpu.VMEM((depth, width), jnp.bfloat16)],
        ),
        compiler_params=VMEM,
        cost_estimate=BRIEF,
    )(meta, *tokens, edges, edges, *weights)


def swiglu_kernel(meta_ref, *refs, base, chunk):
    parts, upstream_ref, out_ref = refs[:SIDE], refs[SIDE], refs[SIDE + 1]
    side = meta_ref[1]
    first = lax.rem(side, 2) == 0
    for count, unit, lane in segments(chunk):
        tile = base + unit + (side if count == SIDE else side // 2)
        width = 2 * LANES * count // SIDE
        summed = parts[0][:, lane : lane + width].astype(jnp.float32)
        for part in parts[1:]:
            summed += part[:, lane : lane + width].astype(jnp.float32)
        lanes = pl.ds(pl.multiple_of(tile * LANES, LANES), LANES)
        incoming = upstream_ref[:, lanes].astype(jnp.float32)
        if count == SIDE:
            gate, upper = summed[:, :LANES], summed[:, LANES:]
        else:
            low = low_half(summed.shape)
            swapped = swap_halves(summed)
            gate = jnp.where(low, summed, swapped)
            upper = jnp.where(low, swapped, summed)
            incoming = jnp.where(low == first, incoming, swap_halves(incoming))
        sigma = jax.nn.sigmoid(gate)
        grad_gate = incoming * upper * sigma * (1.0 + gate * (1.0 - sigma))
        grad_upper = incoming * gate * sigma
        if count == SIDE:
            out_ref[:, lane : lane + LANES] = grad_gate.astype(out_ref.dtype)
            out_ref[:, lane + LANES : lane + width] = grad_upper.astype(out_ref.dtype)
        else:
            value = jnp.where(low, grad_gate, grad_upper)
            out_ref[:, lane : lane + LANES] = value.astype(out_ref.dtype)


def swiglu_backward(meta, parts, upstream, base, chunk):
    rows, width = parts[0].shape
    half = pl.BlockSpec((rows // 2, width), lambda h, m: (h, 0))
    return pl.pallas_call(
        functools.partial(swiglu_kernel, base=base, chunk=chunk),
        out_shape=jax.ShapeDtypeStruct((rows, width), jnp.bfloat16),
        grid_spec=pltpu.PrefetchScalarGridSpec(
            num_scalar_prefetch=1,
            grid=(2,),
            in_specs=[half] * SIDE
            + [
                pl.BlockSpec(
                    (rows // 2, upstream.shape[1]), lambda h, m: (lax.rem(h + m[0], 2), 0)
                )
            ],
            out_specs=half,
        ),
        compiler_params=VMEM,
        cost_estimate=BRIEF,
    )(meta, *parts, upstream)


def backward_kernel(meta_ref, *refs):
    sources = refs[: 2 * SIDE]
    grads = refs[2 * SIDE : 3 * SIDE]
    out_refs = refs[3 * SIDE : 4 * SIDE]
    held, turned, arrived = refs[4 * SIDE :]
    rows = held.shape[2]
    copies = [
        pltpu.make_async_copy(source, held.at[index], arrived.at[index])
        for index, source in enumerate(sources)
    ]
    for step in range(SIDE):
        copies[step].start()
        copies[step + SIDE].start()
    for step, grad in enumerate(grads):
        turned[meta_ref[step]] = grad[...].astype(jnp.float32).T.astype(turned.dtype)
    left = jnp.concatenate(
        [turned[t, :, :rows] for t in range(SIDE)] + [turned[t, :, rows:] for t in range(SIDE)],
        axis=1,
    )
    for step, out_ref in enumerate(out_refs):
        copies[step].wait()
        copies[step + SIDE].wait()
        right = jnp.concatenate(
            [held[step, t] for t in range(SIDE)] + [held[step + SIDE, t] for t in range(SIDE)],
            axis=0,
        )
        total = jnp.dot(left, right, preferred_element_type=jnp.float32)
        out_ref[...] = total.T.astype(out_ref.dtype)


def backward(meta, tokens, grads):
    blocks, rows, features = tokens[0].shape
    width = grads[0].shape[1]
    return pl.pallas_call(
        backward_kernel,
        out_shape=[jax.ShapeDtypeStruct((features, width), jnp.bfloat16)] * SIDE,
        grid_spec=pltpu.PrefetchScalarGridSpec(
            num_scalar_prefetch=1,
            grid=(1,),
            in_specs=[pl.BlockSpec(memory_space=pl.ANY)] * (2 * SIDE)
            + [full((2 * rows, width))] * SIDE,
            out_specs=[full((features, width))] * SIDE,
            scratch_shapes=[
                pltpu.VMEM((2 * SIDE, blocks, rows, features), jnp.bfloat16),
                pltpu.VMEM((SIDE, width, 2 * rows), jnp.bfloat16),
                pltpu.SemaphoreType.DMA((2 * SIDE,)),
            ],
        ),
        compiler_params=VMEM,
        cost_estimate=BRIEF,
    )(meta, *tokens, *grads)


def assemble_kernel(meta_ref, *refs):
    parts = refs[: SIDE * len(CHUNKS)]
    gate_ref, upper_ref, held = refs[SIDE * len(CHUNKS) :]
    side = meta_ref[0]
    base = 0
    for index, chunk in enumerate(CHUNKS):
        pieces = parts[SIDE * index : SIDE * (index + 1)]
        for count, unit, lane in segments(chunk):
            if count == SIDE:
                for step, piece in enumerate(pieces):
                    tile = base + unit + lax.rem(side + step, SIDE)
                    lanes = pl.ds(pl.multiple_of(tile * LANES, LANES), LANES)
                    gate_ref[:, lanes] = piece[:, lane : lane + LANES]
                    upper_ref[:, lanes] = piece[:, lane + LANES : lane + 2 * LANES]
            else:
                for step, piece in enumerate(pieces):
                    value = piece[:, lane : lane + LANES].astype(jnp.float32)
                    held[lax.rem(side + step, SIDE)] = value
                for pair in range(2):
                    left, right = held[2 * pair], held[2 * pair + 1]
                    low = low_half(left.shape)
                    first = (base + unit + pair) * LANES
                    gate = jnp.where(low, left, swap_halves(right))
                    upper = jnp.where(low, swap_halves(left), right)
                    gate_ref[:, first : first + LANES] = gate.astype(gate_ref.dtype)
                    upper_ref[:, first : first + LANES] = upper.astype(upper_ref.dtype)
        base += sum(chunk)


def assemble(meta, pieces, hidden):
    rows = pieces[0].shape[0]
    block = rows // 4
    out = pl.BlockSpec((block, hidden), lambda r, m: (r, 0))
    return pl.pallas_call(
        assemble_kernel,
        out_shape=[jax.ShapeDtypeStruct((rows, hidden), jnp.bfloat16)] * 2,
        grid_spec=pltpu.PrefetchScalarGridSpec(
            num_scalar_prefetch=1,
            grid=(rows // block,),
            in_specs=[
                pl.BlockSpec((block, piece.shape[1]), lambda r, m: (r, 0)) for piece in pieces
            ],
            out_specs=[out, out],
            scratch_shapes=[pltpu.VMEM((SIDE, block, LANES), jnp.float32)],
        ),
        compiler_params=VMEM,
        cost_estimate=BRIEF,
    )(meta, *pieces)


def along_z(value, steps):
    pairs = [
        (z * SIDE + x, (z + steps) % SIDE * SIDE + x) for z in range(SIDE) for x in range(SIDE)
    ]
    return lax.ppermute(value, "fsdp", pairs)


def along_x(value, steps):
    pairs = [
        (z * SIDE + x, z * SIDE + (x + steps) % SIDE) for z in range(SIDE) for x in range(SIDE)
    ]
    return lax.ppermute(value, "fsdp", pairs)


def along_y(value, steps):
    pairs = [(2 * y + c, (y + steps) % SIDE * 2 + c) for y in range(SIDE) for c in range(2)]
    return lax.ppermute(value, "dp", pairs)


def to_sibling(value):
    return lax.ppermute(value, "dp", [(d, d ^ 1) for d in range(2 * SIDE)])


def stacked_over_y(value):
    return jnp.stack([value] + [along_y(value, t) for t in range(1, SIDE)])


def after(value, *earlier):
    return lax.optimization_barrier((value, earlier))[0]


def exchange(slabs):
    return lax.all_to_all(slabs, "dp", split_axis=0, concat_axis=0, tiled=True)


def features_ahead(tokens, spill):
    pairs = [((z + 1) * SIDE, z * SIDE) for z in range(SIDE - 1)]
    return lax.ppermute(tokens[:, :spill], "fsdp", pairs)


def from_first_x(ahead):
    edge = ahead
    for x in range(1, SIDE):
        edge += lax.ppermute(ahead, "fsdp", [(z * SIDE, z * SIDE + x) for z in range(SIDE)])
    return edge


def on_device(old_shards, shard_table, tokens, cotangent):
    n_data = lax.axis_size("dp")
    n_feature = lax.axis_size("fsdp")
    data_index = lax.axis_index("dp")
    feature_index = lax.axis_index("fsdp")
    y, core = data_index // 2, data_index % 2
    z, x = feature_index // SIDE, feature_index % SIDE
    block_rows = tokens.shape[1]
    hidden = cotangent.shape[1]
    row_units = hidden // LANES * n_data
    capacity = old_shards.shape[2]
    first_row = feature_index * block_rows
    slab_rows = pl.cdiv(ALIGN * row_units + capacity, GROUP * row_units) * GROUP
    spill = pl.cdiv(slab_rows, LANES) * LANES
    steps = jnp.arange(SIDE, dtype=jnp.int32)

    matrix_id = data_index // PER_MATRIX
    holder = data_index < 2 * PER_MATRIX
    table_row = (matrix_id * n_feature + feature_index) * PER_MATRIX + data_index % PER_MATRIX
    my_entry = lax.dynamic_index_in_dim(
        shard_table, jnp.minimum(table_row, shard_table.shape[0] - 1), 0, keepdims=False
    )
    lead = (my_entry[0] - first_row * row_units) % (ALIGN * row_units)
    place = jnp.stack([lead, jnp.where(holder, my_entry[1], 0)])
    firsts = shard_table[:, 0].reshape(2, n_feature, PER_MATRIX)
    firsts = lax.dynamic_index_in_dim(firsts, feature_index, 1, keepdims=False).reshape(-1)
    offsets = (firsts // row_units - first_row) // ALIGN * ALIGN
    unpack_meta = jnp.concatenate([offsets, x[None]]).astype(jnp.int32)
    edge_block = 2 * ((z + steps) % SIDE)
    forward_meta = jnp.concatenate(
        [(y - z - steps) % SIDE, (x + 1)[None] % SIDE, edge_block + core, edge_block + 1 - core]
    )
    backward_meta = (y - z + steps) % SIDE

    shard = old_shards[0, 0]
    pack_chunks = functools.partial(
        pack, shard=shard, n_owner=n_data, row_units=row_units, slab_rows=slab_rows
    )
    groups = [[z * SIDE + x for x in range(SIDE)] for z in range(SIDE)]
    outgoing = list(pack_chunks(place, base=0, chunks=CHUNKS[:1]))
    rows = stacked_over_y(tokens)
    ahead = features_ahead(tokens, spill)
    outgoing, rows, ahead, place = lax.optimization_barrier((outgoing, rows, ahead, place))
    incoming = [exchange(outgoing[0])]
    outgoing += list(pack_chunks(place, base=sum(CHUNKS[0]), chunks=CHUNKS[1:]))
    gathered = [rows] + [along_x(rows, s) for s in range(1, SIDE)]
    edge = from_first_x(after(ahead, outgoing[1]))
    edges = lax.all_gather(edge, "dp", axis=0)
    sibling = [to_sibling(part) for part in gathered]
    outgoing, gathered, edge = lax.optimization_barrier((outgoing, gathered, edge))
    gathered = gathered + sibling
    for slabs in outgoing[1:]:
        incoming.append(exchange(after(slabs, incoming[-1])))

    weights, parts, grads, pieces = {}, {}, {}, {}
    latest = outgoing[1]
    for step in ORDER:
        index = int(step[1])
        chunk = CHUNKS[index]
        base = sum(sum(earlier) for earlier in CHUNKS[:index])
        if step[0] == "u":
            slabs = after(incoming[index], latest, sibling)
            columns = unpack(unpack_meta, slabs, block_rows + spill, chunk)
            weights[index] = [columns[0]] + [along_x(columns[s], s) for s in range(1, SIDE)]
            if index == 0:
                upstream = lax.all_gather(
                    after(cotangent, weights[0]), "fsdp", axis=0, tiled=True, axis_index_groups=groups
                )
            latest = columns[0]
        if step[0] == "f":
            own = [after(weights[index][0], latest)] + weights[index][1:]
            partial = forward(forward_meta, gathered, edges, own)
            parts[index] = [partial[0]] + [along_z(partial[s], s) for s in range(1, SIDE)]
            latest = partial[0]
        if step[0] == "s":
            own = [after(parts[index][0], latest)] + parts[index][1:]
            swiglu_meta = jnp.stack([core, x]).astype(jnp.int32)
            latest = swiglu_backward(swiglu_meta, own, upstream, base, chunk)
            grads[index] = [latest] + [along_z(latest, s) for s in range(1, SIDE)]
        if step[0] == "b":
            own = [after(grads[index][0], latest, pieces)] + grads[index][1:]
            sums = backward(backward_meta, gathered, own)
            pieces[index] = [sums[0]] + [along_x(sums[s], -s) for s in range(1, SIDE)]
            latest = sums[0]
    finished = [piece for index in range(len(CHUNKS)) for piece in pieces[index]]
    return tuple(assemble(x[None], finished, hidden))


def solution(mesh):
    return jax.shard_map(
        on_device,
        mesh=mesh,
        in_specs=(P("dp", "fsdp", None, None), P(), P("dp", "fsdp"), P("fsdp", "dp")),
        out_specs=(P("fsdp", "dp"), P("fsdp", "dp")),
        check_vma=False,
    )
```

```python
import functools

import jax
import jax.numpy as jnp
from jax import lax
from jax.experimental import pallas as pl
from jax.experimental.pallas import tpu as pltpu
from jax.sharding import PartitionSpec as P

LANES = 128
GROUP = 176
ALIGN = 8
SIDE = 4
PER_MATRIX = 3
CHUNKS = ((4, 2), (4, 4))
ORDER = ("u0", "f0", "u1", "s0", "f1", "b0", "s1", "b1")
BRIEF = pl.CostEstimate(flops=1, bytes_accessed=1, transcendentals=0)
VMEM = pltpu.CompilerParams(vmem_limit_bytes=32 * 1024 * 1024)


def full(shape):
    return pl.BlockSpec(shape, lambda *_: (0,) * len(shape))


def low_half(shape):
    return lax.broadcasted_iota(jnp.int32, shape, len(shape) - 1) < LANES // 2


def segments(chunk):
    found, unit, lane = [], 0, 0
    for count in chunk:
        found.append((count, unit, lane))
        unit += count
        lane += 2 * LANES * count // SIDE
    return found


def piece_width(chunk):
    return 2 * LANES * sum(chunk) // SIDE


def swap_halves(value):
    return pltpu.roll(value, LANES // 2, value.ndim - 1)


def pack_kernel(place_ref, shard_ref, *refs, row_units, base):
    out_refs, units = refs[:-1], refs[-1]
    group = pl.program_id(0)
    lead = place_ref[0]
    length = place_ref[1]
    block = GROUP * row_units
    held = ALIGN * row_units
    n_owner = out_refs[0].shape[0]
    owned = row_units // n_owner

    @pl.when(group == 0)
    def _():
        units[:held] = jnp.zeros((held, LANES), jnp.float32)

    @pl.when(group > 0)
    def _():
        units[:held] = units[block : block + held]

    whole = (group + 1) * block <= length

    @pl.when(whole)
    def _():
        units[held:] = shard_ref[...].astype(jnp.float32)

    @pl.when(jnp.logical_not(whole))
    def _():
        position = group * block + lax.broadcasted_iota(jnp.int32, (block, LANES), 0)
        units[held:] = jnp.where(position < length, shard_ref[...].astype(jnp.float32), 0.0)

    for owner in range(n_owner):
        column = owner * owned + base
        for out_ref in out_refs:
            for unit in range(out_ref.shape[2] // LANES):
                rows = units[pl.ds(held - lead + column, GROUP, stride=row_units), :]
                out_ref[owner, :, unit * LANES : (unit + 1) * LANES] = rows.astype(out_ref.dtype)
                column += 1


def pack(place, shard, n_owner, row_units, slab_rows, base, chunks):
    block = GROUP * row_units
    last = pl.cdiv(shard.shape[0], block) - 1
    return pl.pallas_call(
        functools.partial(pack_kernel, row_units=row_units, base=base),
        out_shape=[
            jax.ShapeDtypeStruct((n_owner, slab_rows, sum(n) * LANES), shard.dtype) for n in chunks
        ],
        grid_spec=pltpu.PrefetchScalarGridSpec(
            num_scalar_prefetch=1,
            grid=(slab_rows // GROUP,),
            in_specs=[pl.BlockSpec((block, LANES), lambda g, _: (jnp.minimum(g, last), 0))],
            out_specs=[
                pl.BlockSpec((n_owner, GROUP, sum(n) * LANES), lambda g, _: (0, g, 0)) for n in chunks
            ],
            scratch_shapes=[pltpu.VMEM((block + ALIGN * row_units, LANES), jnp.float32)],
        ),
        compiler_params=VMEM,
        cost_estimate=BRIEF,
    )(place, shard)


def unpack_kernel(meta_ref, slab_ref, *refs, chunk):
    out_refs, total = refs[:SIDE], refs[SIDE]
    slab_rows = slab_ref.shape[1]
    side = meta_ref[2 * PER_MATRIX]

    def gathered(matrix, tile):
        total[...] = jnp.zeros_like(total)
        for source in range(matrix * PER_MATRIX, (matrix + 1) * PER_MATRIX):
            rows = pl.ds(pl.multiple_of(meta_ref[source], ALIGN), slab_rows)
            lanes = pl.ds(pl.multiple_of(tile * LANES, LANES), LANES)
            total[rows, :] += slab_ref[source, :, lanes].astype(jnp.float32)
        return total[...]

    for step, out_ref in enumerate(out_refs):
        part = lax.rem(side + step, SIDE)
        for count, unit, lane in segments(chunk):
            if count == SIDE:
                for matrix in range(2):
                    lanes = slice(lane + matrix * LANES, lane + (matrix + 1) * LANES)
                    out_ref[:, lanes] = gathered(matrix, unit + part).astype(out_ref.dtype)
            else:
                first = lax.rem(part, 2) == 0
                gate = gathered(0, unit + part // 2)
                gate = jnp.where(first, gate, swap_halves(gate))
                upper = gathered(1, unit + part // 2)
                upper = jnp.where(first, swap_halves(upper), upper)
                value = jnp.where(low_half(gate.shape), gate, upper)
                out_ref[:, lane : lane + LANES] = value.astype(out_ref.dtype)


def unpack(meta, slabs, rows_out, chunk):
    _, slab_rows, width = slabs.shape
    out_width = piece_width(chunk)
    sources = 2 * PER_MATRIX
    return pl.pallas_call(
        functools.partial(unpack_kernel, chunk=chunk),
        out_shape=[jax.ShapeDtypeStruct((rows_out, out_width), slabs.dtype)] * SIDE,
        grid_spec=pltpu.PrefetchScalarGridSpec(
            num_scalar_prefetch=1,
            grid=(1,),
            in_specs=[full((sources, slab_rows, width))],
            out_specs=[full((rows_out, out_width))] * SIDE,
            scratch_shapes=[pltpu.VMEM((rows_out, LANES), jnp.float32)],
        ),
        compiler_params=VMEM,
        cost_estimate=BRIEF,
    )(meta, slabs)


def forward_kernel(meta_ref, *refs):
    own, sibling = refs[:SIDE], refs[SIDE : 2 * SIDE]
    edges = refs[2 * SIDE : 2 * SIDE + 2]
    weights = refs[2 * SIDE + 2 : 3 * SIDE + 2]
    out_refs = refs[3 * SIDE + 2 : 4 * SIDE + 2]
    joined = refs[4 * SIDE + 2]
    piece = pl.program_id(0)
    last = meta_ref[SIDE]
    features = own[0].shape[2]
    spill = weights[0].shape[0] - features
    rows = own[0].shape[1]

    @pl.when(piece == 0)
    def _():
        beyond = None
        for step, weight in enumerate(weights):
            source = (step + 1) % SIDE
            tail = weights[source][features:].astype(jnp.float32)
            inside = jnp.where(last == source, 0.0, tail)
            outside = tail - inside
            beyond = outside if beyond is None else beyond + outside
            head = weight[:spill].astype(jnp.float32) + inside
            first = step * features
            joined[first : first + spill] = head.astype(joined.dtype)
            joined[first + spill : first + features] = weight[spill:features]
        first = SIDE * features
        joined[first : first + spill] = beyond.astype(joined.dtype)
        rest = joined.shape[0] - first - spill
        joined[first + spill :] = jnp.zeros((rest, joined.shape[1]), joined.dtype)

    for half, (parts, edge) in enumerate(((own, edges[0]), (sibling, edges[1]))):
        left = jnp.concatenate([part[0] for part in parts] + [edge[0]], axis=1)
        value = jnp.dot(left, joined[...], preferred_element_type=jnp.float32)
        value = value.astype(jnp.bfloat16)
        for index, out_ref in enumerate(out_refs):

            @pl.when(piece == index)
            def _():
                out_ref[half * rows : (half + 1) * rows] = value


def forward(meta, tokens, edges, weights):
    _, rows, features = tokens[0].shape
    spill = edges.shape[2]
    width = weights[0].shape[1]
    depth = SIDE * features + spill
    block = pl.BlockSpec((1, rows, features), lambda p, m: (m[p], 0, 0))
    edge = lambda first: pl.BlockSpec((1, rows, spill), lambda p, m: (m[first + p], 0, 0))
    return pl.pallas_call(
        forward_kernel,
        out_shape=[jax.ShapeDtypeStruct((2 * rows, width), jnp.bfloat16)] * SIDE,
        grid_spec=pltpu.PrefetchScalarGridSpec(
            num_scalar_prefetch=1,
            grid=(SIDE,),
            in_specs=[block] * (2 * SIDE)
            + [edge(SIDE + 1), edge(2 * SIDE + 1)]
            + [full(weights[0].shape)] * SIDE,
            out_specs=[full((2 * rows, width))] * SIDE,
            scratch_shapes=[pltpu.VMEM((depth, width), jnp.bfloat16)],
        ),
        compiler_params=VMEM,
        cost_estimate=BRIEF,
    )(meta, *tokens, edges, edges, *weights)


def swiglu_kernel(meta_ref, *refs, base, chunk):
    parts, upstream_ref, out_ref = refs[:SIDE], refs[SIDE], refs[SIDE + 1]
    side = meta_ref[1]
    first = lax.rem(side, 2) == 0
    for count, unit, lane in segments(chunk):
        tile = base + unit + (side if count == SIDE else side // 2)
        width = 2 * LANES * count // SIDE
        summed = parts[0][:, lane : lane + width].astype(jnp.float32)
        for part in parts[1:]:
            summed += part[:, lane : lane + width].astype(jnp.float32)
        lanes = pl.ds(pl.multiple_of(tile * LANES, LANES), LANES)
        incoming = upstream_ref[:, lanes].astype(jnp.float32)
        if count == SIDE:
            gate, upper = summed[:, :LANES], summed[:, LANES:]
        else:
            low = low_half(summed.shape)
            swapped = swap_halves(summed)
            gate = jnp.where(low, summed, swapped)
            upper = jnp.where(low, swapped, summed)
            incoming = jnp.where(low == first, incoming, swap_halves(incoming))
        sigma = jax.nn.sigmoid(gate)
        grad_gate = incoming * upper * sigma * (1.0 + gate * (1.0 - sigma))
        grad_upper = incoming * gate * sigma
        if count == SIDE:
            out_ref[:, lane : lane + LANES] = grad_gate.astype(out_ref.dtype)
            out_ref[:, lane + LANES : lane + width] = grad_upper.astype(out_ref.dtype)
        else:
            value = jnp.where(low, grad_gate, grad_upper)
            out_ref[:, lane : lane + LANES] = value.astype(out_ref.dtype)


def swiglu_backward(meta, parts, upstream, base, chunk):
    rows, width = parts[0].shape
    half = pl.BlockSpec((rows // 2, width), lambda h, m: (h, 0))
    return pl.pallas_call(
        functools.partial(swiglu_kernel, base=base, chunk=chunk),
        out_shape=jax.ShapeDtypeStruct((rows, width), jnp.bfloat16),
        grid_spec=pltpu.PrefetchScalarGridSpec(
            num_scalar_prefetch=1,
            grid=(2,),
            in_specs=[half] * SIDE
            + [
                pl.BlockSpec(
                    (rows // 2, upstream.shape[1]), lambda h, m: (lax.rem(h + m[0], 2), 0)
                )
            ],
            out_specs=half,
        ),
        compiler_params=VMEM,
        cost_estimate=BRIEF,
    )(meta, *parts, upstream)


def backward_kernel(meta_ref, *refs):
    sources = refs[: 2 * SIDE]
    grads = refs[2 * SIDE : 3 * SIDE]
    out_refs = refs[3 * SIDE : 4 * SIDE]
    held, turned, arrived = refs[4 * SIDE :]
    rows = held.shape[2]
    copies = [
        pltpu.make_async_copy(source, held.at[index], arrived.at[index])
        for index, source in enumerate(sources)
    ]
    for step in range(SIDE):
        copies[step].start()
        copies[step + SIDE].start()
    for step, grad in enumerate(grads):
        turned[meta_ref[step]] = grad[...].astype(jnp.float32).T.astype(turned.dtype)
    left = jnp.concatenate(
        [turned[t, :, :rows] for t in range(SIDE)] + [turned[t, :, rows:] for t in range(SIDE)],
        axis=1,
    )
    for step, out_ref in enumerate(out_refs):
        copies[step].wait()
        copies[step + SIDE].wait()
        right = jnp.concatenate(
            [held[step, t] for t in range(SIDE)] + [held[step + SIDE, t] for t in range(SIDE)],
            axis=0,
        )
        total = jnp.dot(left, right, preferred_element_type=jnp.float32)
        out_ref[...] = total.T.astype(out_ref.dtype)


def backward(meta, tokens, grads):
    blocks, rows, features = tokens[0].shape
    width = grads[0].shape[1]
    return pl.pallas_call(
        backward_kernel,
        out_shape=[jax.ShapeDtypeStruct((features, width), jnp.bfloat16)] * SIDE,
        grid_spec=pltpu.PrefetchScalarGridSpec(
            num_scalar_prefetch=1,
            grid=(1,),
            in_specs=[pl.BlockSpec(memory_space=pl.ANY)] * (2 * SIDE)
            + [full((2 * rows, width))] * SIDE,
            out_specs=[full((features, width))] * SIDE,
            scratch_shapes=[
                pltpu.VMEM((2 * SIDE, blocks, rows, features), jnp.bfloat16),
                pltpu.VMEM((SIDE, width, 2 * rows), jnp.bfloat16),
                pltpu.SemaphoreType.DMA((2 * SIDE,)),
            ],
        ),
        compiler_params=VMEM,
        cost_estimate=BRIEF,
    )(meta, *tokens, *grads)


def assemble_kernel(meta_ref, *refs):
    parts = refs[: SIDE * len(CHUNKS)]
    gate_ref, upper_ref, held = refs[SIDE * len(CHUNKS) :]
    side = meta_ref[0]
    base = 0
    for index, chunk in enumerate(CHUNKS):
        pieces = parts[SIDE * index : SIDE * (index + 1)]
        for count, unit, lane in segments(chunk):
            if count == SIDE:
                for step, piece in enumerate(pieces):
                    tile = base + unit + lax.rem(side + step, SIDE)
                    lanes = pl.ds(pl.multiple_of(tile * LANES, LANES), LANES)
                    gate_ref[:, lanes] = piece[:, lane : lane + LANES]
                    upper_ref[:, lanes] = piece[:, lane + LANES : lane + 2 * LANES]
            else:
                for step, piece in enumerate(pieces):
                    value = piece[:, lane : lane + LANES].astype(jnp.float32)
                    held[lax.rem(side + step, SIDE)] = value
                for pair in range(2):
                    left, right = held[2 * pair], held[2 * pair + 1]
                    low = low_half(left.shape)
                    first = (base + unit + pair) * LANES
                    gate = jnp.where(low, left, swap_halves(right))
                    upper = jnp.where(low, swap_halves(left), right)
                    gate_ref[:, first : first + LANES] = gate.astype(gate_ref.dtype)
                    upper_ref[:, first : first + LANES] = upper.astype(upper_ref.dtype)
        base += sum(chunk)


def assemble(meta, pieces, hidden):
    rows = pieces[0].shape[0]
    block = rows // 4
    out = pl.BlockSpec((block, hidden), lambda r, m: (r, 0))
    return pl.pallas_call(
        assemble_kernel,
        out_shape=[jax.ShapeDtypeStruct((rows, hidden), jnp.bfloat16)] * 2,
        grid_spec=pltpu.PrefetchScalarGridSpec(
            num_scalar_prefetch=1,
            grid=(rows // block,),
            in_specs=[
                pl.BlockSpec((block, piece.shape[1]), lambda r, m: (r, 0)) for piece in pieces
            ],
            out_specs=[out, out],
            scratch_shapes=[pltpu.VMEM((SIDE, block, LANES), jnp.float32)],
        ),
        compiler_params=VMEM,
        cost_estimate=BRIEF,
    )(meta, *pieces)


def along_z(value, steps):
    pairs = [
        (z * SIDE + x, (z + steps) % SIDE * SIDE + x) for z in range(SIDE) for x in range(SIDE)
    ]
    return lax.ppermute(value, "fsdp", pairs)


def along_x(value, steps):
    pairs = [
        (z * SIDE + x, z * SIDE + (x + steps) % SIDE) for z in range(SIDE) for x in range(SIDE)
    ]
    return lax.ppermute(value, "fsdp", pairs)


def along_y(value, steps):
    pairs = [(2 * y + c, (y + steps) % SIDE * 2 + c) for y in range(SIDE) for c in range(2)]
    return lax.ppermute(value, "dp", pairs)


def to_sibling(value):
    return lax.ppermute(value, "dp", [(d, d ^ 1) for d in range(2 * SIDE)])


def stacked_over_y(value):
    return jnp.stack([value] + [along_y(value, t) for t in range(1, SIDE)])


def after(value, *earlier):
    return lax.optimization_barrier((value, earlier))[0]


def exchange(slabs):
    return lax.all_to_all(slabs, "dp", split_axis=0, concat_axis=0, tiled=True)


def features_ahead(tokens, spill):
    pairs = [((z + 1) * SIDE, z * SIDE) for z in range(SIDE - 1)]
    return lax.ppermute(tokens[:, :spill], "fsdp", pairs)


def from_first_x(ahead):
    edge = ahead
    for x in range(1, SIDE):
        edge += lax.ppermute(ahead, "fsdp", [(z * SIDE, z * SIDE + x) for z in range(SIDE)])
    return edge


def on_device(old_shards, shard_table, tokens, cotangent):
    n_data = lax.axis_size("dp")
    n_feature = lax.axis_size("fsdp")
    data_index = lax.axis_index("dp")
    feature_index = lax.axis_index("fsdp")
    y, core = data_index // 2, data_index % 2
    z, x = feature_index // SIDE, feature_index % SIDE
    block_rows = tokens.shape[1]
    hidden = cotangent.shape[1]
    row_units = hidden // LANES * n_data
    capacity = old_shards.shape[2]
    first_row = feature_index * block_rows
    slab_rows = pl.cdiv(ALIGN * row_units + capacity, GROUP * row_units) * GROUP
    spill = pl.cdiv(slab_rows, LANES) * LANES
    steps = jnp.arange(SIDE, dtype=jnp.int32)

    matrix_id = data_index // PER_MATRIX
    holder = data_index < 2 * PER_MATRIX
    table_row = (matrix_id * n_feature + feature_index) * PER_MATRIX + data_index % PER_MATRIX
    my_entry = lax.dynamic_index_in_dim(
        shard_table, jnp.minimum(table_row, shard_table.shape[0] - 1), 0, keepdims=False
    )
    lead = (my_entry[0] - first_row * row_units) % (ALIGN * row_units)
    place = jnp.stack([lead, jnp.where(holder, my_entry[1], 0)])
    firsts = shard_table[:, 0].reshape(2, n_feature, PER_MATRIX)
    firsts = lax.dynamic_index_in_dim(firsts, feature_index, 1, keepdims=False).reshape(-1)
    offsets = (firsts // row_units - first_row) // ALIGN * ALIGN
    unpack_meta = jnp.concatenate([offsets, x[None]]).astype(jnp.int32)
    edge_block = 2 * ((z + steps) % SIDE)
    forward_meta = jnp.concatenate(
        [(y - z - steps) % SIDE, (x + 1)[None] % SIDE, edge_block + core, edge_block + 1 - core]
    )
    backward_meta = (y - z + steps) % SIDE
    swiglu_meta = jnp.stack([core, x]).astype(jnp.int32)

    shard = old_shards[0, 0]
    pack_chunks = functools.partial(
        pack, shard=shard, n_owner=n_data, row_units=row_units, slab_rows=slab_rows
    )
    groups = [[z * SIDE + x for x in range(SIDE)] for z in range(SIDE)]
    outgoing = list(pack_chunks(place, base=0, chunks=CHUNKS[:1]))
    rows = stacked_over_y(tokens)
    edge = from_first_x(features_ahead(tokens, spill))
    outgoing, rows, edge, place = lax.optimization_barrier((outgoing, rows, edge, place))
    incoming = [exchange(outgoing[0])]
    outgoing += list(pack_chunks(place, base=sum(CHUNKS[0]), chunks=CHUNKS[1:]))
    gathered = [rows] + [along_x(rows, s) for s in range(1, SIDE)]
    edges = lax.all_gather(edge, "dp", axis=0)
    sibling = [to_sibling(part) for part in gathered]
    outgoing, gathered, edges, unpack_meta, forward_meta, backward_meta, swiglu_meta = (
        lax.optimization_barrier(
            (outgoing, gathered, edges, unpack_meta, forward_meta, backward_meta, swiglu_meta)
        )
    )
    gathered = gathered + sibling
    for slabs in outgoing[1:]:
        incoming.append(exchange(after(slabs, incoming[-1])))

    weights, parts, grads, pieces = {}, {}, {}, {}
    latest = outgoing[1]
    for step in ORDER:
        index = int(step[1])
        chunk = CHUNKS[index]
        base = sum(sum(earlier) for earlier in CHUNKS[:index])
        if step[0] == "u":
            slabs = after(incoming[index], latest)
            columns = unpack(unpack_meta, slabs, block_rows + slab_rows, chunk)
            weights[index] = [columns[0]] + [along_x(columns[s], s) for s in range(1, SIDE)]
            if index == 0:
                source = after(cotangent, weights[0])
                upstream = lax.all_gather(
                    source, "fsdp", axis=0, tiled=True, axis_index_groups=groups
                )
            latest = columns[0]
        if step[0] == "f":
            own = [after(weights[index][0], latest)] + weights[index][1:]
            partial = forward(forward_meta, gathered, edges, own)
            parts[index] = [partial[0]] + [along_z(partial[s], s) for s in range(1, SIDE)]
            latest = partial[0]
        if step[0] == "s":
            own = [after(parts[index][0], latest)] + parts[index][1:]
            latest = swiglu_backward(swiglu_meta, own, upstream, base, chunk)
            grads[index] = [latest] + [along_z(latest, s) for s in range(1, SIDE)]
        if step[0] == "b":
            own = [after(grads[index][0], latest, pieces)] + grads[index][1:]
            sums = backward(backward_meta, gathered, own)
            pieces[index] = [sums[0]] + [along_x(sums[s], -s) for s in range(1, SIDE)]
            latest = sums[0]
    finished = [piece for index in range(len(CHUNKS)) for piece in pieces[index]]
    return tuple(assemble(x[None], finished, hidden))


def solution(mesh):
    return jax.shard_map(
        on_device,
        mesh=mesh,
        in_specs=(P("dp", "fsdp", None, None), P(), P("dp", "fsdp"), P("fsdp", "dp")),
        out_specs=(P("fsdp", "dp"), P("fsdp", "dp")),
        check_vma=False,
    )
```

```python
import functools

import jax
import jax.numpy as jnp
from jax import lax
from jax.experimental import pallas as pl
from jax.experimental.pallas import tpu as pltpu
from jax.sharding import PartitionSpec as P

LANES = 128
GROUP = 176
ALIGN = 8
SIDE = 4
PER_MATRIX = 3
CHUNKS = ((4, 2), (4, 4))
ORDER = ("u0", "f0", "u1", "s0", "f1", "b0", "s1", "b1")
BRIEF = pl.CostEstimate(flops=1, bytes_accessed=1, transcendentals=0)
VMEM = pltpu.CompilerParams(vmem_limit_bytes=32 * 1024 * 1024)


def full(shape):
    return pl.BlockSpec(shape, lambda *_: (0,) * len(shape))


def low_half(shape):
    return lax.broadcasted_iota(jnp.int32, shape, len(shape) - 1) < LANES // 2


def segments(chunk):
    found, unit, lane = [], 0, 0
    for count in chunk:
        found.append((count, unit, lane))
        unit += count
        lane += 2 * LANES * count // SIDE
    return found


def piece_width(chunk):
    return 2 * LANES * sum(chunk) // SIDE


def swap_halves(value):
    return pltpu.roll(value, LANES // 2, value.ndim - 1)


def pack_kernel(place_ref, shard_ref, *refs, row_units, base):
    out_refs, units = refs[:-1], refs[-1]
    group = pl.program_id(0)
    lead = place_ref[0]
    length = place_ref[1]
    block = GROUP * row_units
    held = ALIGN * row_units
    n_owner = out_refs[0].shape[0]
    owned = row_units // n_owner

    @pl.when(group == 0)
    def _():
        units[:held] = jnp.zeros((held, LANES), jnp.float32)

    @pl.when(group > 0)
    def _():
        units[:held] = units[block : block + held]

    whole = (group + 1) * block <= length

    @pl.when(whole)
    def _():
        units[held:] = shard_ref[...].astype(jnp.float32)

    @pl.when(jnp.logical_not(whole))
    def _():
        position = group * block + lax.broadcasted_iota(jnp.int32, (block, LANES), 0)
        units[held:] = jnp.where(position < length, shard_ref[...].astype(jnp.float32), 0.0)

    for owner in range(n_owner):
        column = owner * owned + base
        for out_ref in out_refs:
            for unit in range(out_ref.shape[2] // LANES):
                rows = units[pl.ds(held - lead + column, GROUP, stride=row_units), :]
                out_ref[owner, :, unit * LANES : (unit + 1) * LANES] = rows.astype(out_ref.dtype)
                column += 1


def pack(place, shard, n_owner, row_units, slab_rows, base, chunks):
    block = GROUP * row_units
    last = pl.cdiv(shard.shape[0], block) - 1
    return pl.pallas_call(
        functools.partial(pack_kernel, row_units=row_units, base=base),
        out_shape=[
            jax.ShapeDtypeStruct((n_owner, slab_rows, sum(n) * LANES), shard.dtype) for n in chunks
        ],
        grid_spec=pltpu.PrefetchScalarGridSpec(
            num_scalar_prefetch=1,
            grid=(slab_rows // GROUP,),
            in_specs=[pl.BlockSpec((block, LANES), lambda g, _: (jnp.minimum(g, last), 0))],
            out_specs=[
                pl.BlockSpec((n_owner, GROUP, sum(n) * LANES), lambda g, _: (0, g, 0)) for n in chunks
            ],
            scratch_shapes=[pltpu.VMEM((block + ALIGN * row_units, LANES), jnp.float32)],
        ),
        compiler_params=VMEM,
        cost_estimate=BRIEF,
    )(place, shard)


def unpack_kernel(meta_ref, slab_ref, *refs, chunk):
    out_refs, total = refs[:SIDE], refs[SIDE]
    slab_rows = slab_ref.shape[1]
    side = meta_ref[2 * PER_MATRIX]

    def gathered(matrix, tile):
        total[...] = jnp.zeros_like(total)
        for source in range(matrix * PER_MATRIX, (matrix + 1) * PER_MATRIX):
            rows = pl.ds(pl.multiple_of(meta_ref[source], ALIGN), slab_rows)
            lanes = pl.ds(pl.multiple_of(tile * LANES, LANES), LANES)
            total[rows, :] += slab_ref[source, :, lanes].astype(jnp.float32)
        return total[...]

    for step, out_ref in enumerate(out_refs):
        part = lax.rem(side + step, SIDE)
        for count, unit, lane in segments(chunk):
            if count == SIDE:
                for matrix in range(2):
                    lanes = slice(lane + matrix * LANES, lane + (matrix + 1) * LANES)
                    out_ref[:, lanes] = gathered(matrix, unit + part).astype(out_ref.dtype)
            else:
                first = lax.rem(part, 2) == 0
                gate = gathered(0, unit + part // 2)
                gate = jnp.where(first, gate, swap_halves(gate))
                upper = gathered(1, unit + part // 2)
                upper = jnp.where(first, swap_halves(upper), upper)
                value = jnp.where(low_half(gate.shape), gate, upper)
                out_ref[:, lane : lane + LANES] = value.astype(out_ref.dtype)


def unpack(meta, slabs, rows_out, chunk):
    _, slab_rows, width = slabs.shape
    out_width = piece_width(chunk)
    sources = 2 * PER_MATRIX
    return pl.pallas_call(
        functools.partial(unpack_kernel, chunk=chunk),
        out_shape=[jax.ShapeDtypeStruct((rows_out, out_width), slabs.dtype)] * SIDE,
        grid_spec=pltpu.PrefetchScalarGridSpec(
            num_scalar_prefetch=1,
            grid=(1,),
            in_specs=[full((sources, slab_rows, width))],
            out_specs=[full((rows_out, out_width))] * SIDE,
            scratch_shapes=[pltpu.VMEM((rows_out, LANES), jnp.float32)],
        ),
        compiler_params=VMEM,
        cost_estimate=BRIEF,
    )(meta, slabs)


def forward_kernel(meta_ref, *refs):
    own, sibling = refs[:SIDE], refs[SIDE : 2 * SIDE]
    edges = refs[2 * SIDE : 2 * SIDE + 2]
    weights = refs[2 * SIDE + 2 : 3 * SIDE + 2]
    out_refs = refs[3 * SIDE + 2 : 4 * SIDE + 2]
    joined = refs[4 * SIDE + 2]
    piece = pl.program_id(0)
    last = meta_ref[SIDE]
    features = own[0].shape[2]
    spill = weights[0].shape[0] - features
    rows = own[0].shape[1]

    @pl.when(piece == 0)
    def _():
        beyond = None
        for step, weight in enumerate(weights):
            source = (step + 1) % SIDE
            tail = weights[source][features:].astype(jnp.float32)
            inside = jnp.where(last == source, 0.0, tail)
            outside = tail - inside
            beyond = outside if beyond is None else beyond + outside
            head = weight[:spill].astype(jnp.float32) + inside
            first = step * features
            joined[first : first + spill] = head.astype(joined.dtype)
            joined[first + spill : first + features] = weight[spill:features]
        first = SIDE * features
        joined[first : first + spill] = beyond.astype(joined.dtype)
        rest = joined.shape[0] - first - spill
        joined[first + spill :] = jnp.zeros((rest, joined.shape[1]), joined.dtype)

    for half, (parts, edge) in enumerate(((own, edges[0]), (sibling, edges[1]))):
        left = jnp.concatenate([part[0] for part in parts] + [edge[0]], axis=1)
        value = jnp.dot(left, joined[...], preferred_element_type=jnp.float32)
        value = value.astype(jnp.bfloat16)
        for index, out_ref in enumerate(out_refs):

            @pl.when(piece == index)
            def _():
                out_ref[half * rows : (half + 1) * rows] = value


def forward(meta, tokens, edges, weights):
    _, rows, features = tokens[0].shape
    spill = edges.shape[2]
    width = weights[0].shape[1]
    depth = SIDE * features + spill
    block = pl.BlockSpec((1, rows, features), lambda p, m: (m[p], 0, 0))
    edge = lambda first: pl.BlockSpec((1, rows, spill), lambda p, m: (m[first + p], 0, 0))
    return pl.pallas_call(
        forward_kernel,
        out_shape=[jax.ShapeDtypeStruct((2 * rows, width), jnp.bfloat16)] * SIDE,
        grid_spec=pltpu.PrefetchScalarGridSpec(
            num_scalar_prefetch=1,
            grid=(SIDE,),
            in_specs=[block] * (2 * SIDE)
            + [edge(SIDE + 1), edge(2 * SIDE + 1)]
            + [full(weights[0].shape)] * SIDE,
            out_specs=[full((2 * rows, width))] * SIDE,
            scratch_shapes=[pltpu.VMEM((depth, width), jnp.bfloat16)],
        ),
        compiler_params=VMEM,
        cost_estimate=BRIEF,
    )(meta, *tokens, edges, edges, *weights)


def swiglu_kernel(meta_ref, *refs, base, chunk):
    parts, upstream_ref, out_ref = refs[:SIDE], refs[SIDE], refs[SIDE + 1]
    side = meta_ref[1]
    first = lax.rem(side, 2) == 0
    for count, unit, lane in segments(chunk):
        tile = base + unit + (side if count == SIDE else side // 2)
        width = 2 * LANES * count // SIDE
        summed = parts[0][:, lane : lane + width].astype(jnp.float32)
        for part in parts[1:]:
            summed += part[:, lane : lane + width].astype(jnp.float32)
        lanes = pl.ds(pl.multiple_of(tile * LANES, LANES), LANES)
        incoming = upstream_ref[:, lanes].astype(jnp.float32)
        if count == SIDE:
            gate, upper = summed[:, :LANES], summed[:, LANES:]
        else:
            low = low_half(summed.shape)
            swapped = swap_halves(summed)
            gate = jnp.where(low, summed, swapped)
            upper = jnp.where(low, swapped, summed)
            incoming = jnp.where(low == first, incoming, swap_halves(incoming))
        sigma = jax.nn.sigmoid(gate)
        grad_gate = incoming * upper * sigma * (1.0 + gate * (1.0 - sigma))
        grad_upper = incoming * gate * sigma
        if count == SIDE:
            out_ref[:, lane : lane + LANES] = grad_gate.astype(out_ref.dtype)
            out_ref[:, lane + LANES : lane + width] = grad_upper.astype(out_ref.dtype)
        else:
            value = jnp.where(low, grad_gate, grad_upper)
            out_ref[:, lane : lane + LANES] = value.astype(out_ref.dtype)


def swiglu_backward(meta, parts, upstream, base, chunk):
    rows, width = parts[0].shape
    half = pl.BlockSpec((rows // 2, width), lambda h, m: (h, 0))
    return pl.pallas_call(
        functools.partial(swiglu_kernel, base=base, chunk=chunk),
        out_shape=jax.ShapeDtypeStruct((rows, width), jnp.bfloat16),
        grid_spec=pltpu.PrefetchScalarGridSpec(
            num_scalar_prefetch=1,
            grid=(2,),
            in_specs=[half] * SIDE
            + [
                pl.BlockSpec(
                    (rows // 2, upstream.shape[1]), lambda h, m: (lax.rem(h + m[0], 2), 0)
                )
            ],
            out_specs=half,
        ),
        compiler_params=VMEM,
        cost_estimate=BRIEF,
    )(meta, *parts, upstream)


def backward_kernel(meta_ref, *refs, count):
    sources = refs[: 2 * SIDE]
    grads = refs[2 * SIDE : 2 * SIDE + count]
    out_refs = refs[2 * SIDE + count : 3 * SIDE + count]
    held, turned, arrived = refs[3 * SIDE + count :]
    rows = held.shape[2]
    copies = [
        pltpu.make_async_copy(source, held.at[index], arrived.at[index])
        for index, source in enumerate(sources)
    ]
    for step in range(SIDE):
        copies[step].start()
        copies[step + SIDE].start()
    for step, grad in zip((0, 1, 3), grads):
        turned[meta_ref[step]] = grad[...].astype(jnp.float32).T.astype(turned.dtype)
    first = 0
    for grad in grads[3:]:
        lanes = slice(first, first + grad.shape[0])
        turned[meta_ref[2], :, lanes] = grad[...].astype(jnp.float32).T.astype(turned.dtype)
        first += grad.shape[0]
    left = jnp.concatenate(
        [turned[t, :, :rows] for t in range(SIDE)] + [turned[t, :, rows:] for t in range(SIDE)],
        axis=1,
    )
    for step, out_ref in enumerate(out_refs):
        copies[step].wait()
        copies[step + SIDE].wait()
        right = jnp.concatenate(
            [held[step, t] for t in range(SIDE)] + [held[step + SIDE, t] for t in range(SIDE)],
            axis=0,
        )
        total = jnp.dot(left, right, preferred_element_type=jnp.float32)
        out_ref[...] = total.T.astype(out_ref.dtype)


def backward(meta, tokens, grads):
    blocks, rows, features = tokens[0].shape
    width = grads[0].shape[1]
    return pl.pallas_call(
        functools.partial(backward_kernel, count=len(grads)),
        out_shape=[jax.ShapeDtypeStruct((features, width), jnp.bfloat16)] * SIDE,
        grid_spec=pltpu.PrefetchScalarGridSpec(
            num_scalar_prefetch=1,
            grid=(1,),
            in_specs=[pl.BlockSpec(memory_space=pl.ANY)] * (2 * SIDE)
            + [full(grad.shape) for grad in grads],
            out_specs=[full((features, width))] * SIDE,
            scratch_shapes=[
                pltpu.VMEM((2 * SIDE, blocks, rows, features), jnp.bfloat16),
                pltpu.VMEM((SIDE, width, 2 * rows), jnp.bfloat16),
                pltpu.SemaphoreType.DMA((2 * SIDE,)),
            ],
        ),
        compiler_params=VMEM,
        cost_estimate=BRIEF,
    )(meta, *tokens, *grads)


def assemble_kernel(meta_ref, *refs):
    parts = refs[: SIDE * len(CHUNKS)]
    gate_ref, upper_ref, held = refs[SIDE * len(CHUNKS) :]
    side = meta_ref[0]
    base = 0
    for index, chunk in enumerate(CHUNKS):
        pieces = parts[SIDE * index : SIDE * (index + 1)]
        for count, unit, lane in segments(chunk):
            if count == SIDE:
                for step, piece in enumerate(pieces):
                    tile = base + unit + lax.rem(side + step, SIDE)
                    lanes = pl.ds(pl.multiple_of(tile * LANES, LANES), LANES)
                    gate_ref[:, lanes] = piece[:, lane : lane + LANES]
                    upper_ref[:, lanes] = piece[:, lane + LANES : lane + 2 * LANES]
            else:
                for step, piece in enumerate(pieces):
                    value = piece[:, lane : lane + LANES].astype(jnp.float32)
                    held[lax.rem(side + step, SIDE)] = value
                for pair in range(2):
                    left, right = held[2 * pair], held[2 * pair + 1]
                    low = low_half(left.shape)
                    first = (base + unit + pair) * LANES
                    gate = jnp.where(low, left, swap_halves(right))
                    upper = jnp.where(low, swap_halves(left), right)
                    gate_ref[:, first : first + LANES] = gate.astype(gate_ref.dtype)
                    upper_ref[:, first : first + LANES] = upper.astype(upper_ref.dtype)
        base += sum(chunk)


def assemble(meta, pieces, hidden):
    rows = pieces[0].shape[0]
    block = rows // 4
    out = pl.BlockSpec((block, hidden), lambda r, m: (r, 0))
    return pl.pallas_call(
        assemble_kernel,
        out_shape=[jax.ShapeDtypeStruct((rows, hidden), jnp.bfloat16)] * 2,
        grid_spec=pltpu.PrefetchScalarGridSpec(
            num_scalar_prefetch=1,
            grid=(rows // block,),
            in_specs=[
                pl.BlockSpec((block, piece.shape[1]), lambda r, m: (r, 0)) for piece in pieces
            ],
            out_specs=[out, out],
            scratch_shapes=[pltpu.VMEM((SIDE, block, LANES), jnp.float32)],
        ),
        compiler_params=VMEM,
        cost_estimate=BRIEF,
    )(meta, *pieces)


def along_z(value, steps):
    pairs = [
        (z * SIDE + x, (z + steps) % SIDE * SIDE + x) for z in range(SIDE) for x in range(SIDE)
    ]
    return lax.ppermute(value, "fsdp", pairs)


def along_x(value, steps):
    pairs = [
        (z * SIDE + x, z * SIDE + (x + steps) % SIDE) for z in range(SIDE) for x in range(SIDE)
    ]
    return lax.ppermute(value, "fsdp", pairs)


def along_y(value, steps):
    pairs = [(2 * y + c, (y + steps) % SIDE * 2 + c) for y in range(SIDE) for c in range(2)]
    return lax.ppermute(value, "dp", pairs)


def to_sibling(value):
    return lax.ppermute(value, "dp", [(d, d ^ 1) for d in range(2 * SIDE)])


def stacked_over_y(value):
    return jnp.stack([value] + [along_y(value, t) for t in range(1, SIDE)])


def after(value, *earlier):
    return lax.optimization_barrier((value, earlier))[0]


def exchange(slabs):
    return lax.all_to_all(slabs, "dp", split_axis=0, concat_axis=0, tiled=True)


def features_ahead(tokens, spill):
    pairs = [((z + 1) * SIDE, z * SIDE) for z in range(SIDE - 1)]
    return lax.ppermute(tokens[:, :spill], "fsdp", pairs)


def from_first_x(ahead):
    edge = ahead
    for x in range(1, SIDE):
        edge += lax.ppermute(ahead, "fsdp", [(z * SIDE, z * SIDE + x) for z in range(SIDE)])
    return edge


def on_device(old_shards, shard_table, tokens, cotangent):
    n_data = lax.axis_size("dp")
    n_feature = lax.axis_size("fsdp")
    data_index = lax.axis_index("dp")
    feature_index = lax.axis_index("fsdp")
    y, core = data_index // 2, data_index % 2
    z, x = feature_index // SIDE, feature_index % SIDE
    block_rows = tokens.shape[1]
    hidden = cotangent.shape[1]
    row_units = hidden // LANES * n_data
    capacity = old_shards.shape[2]
    first_row = feature_index * block_rows
    slab_rows = pl.cdiv(ALIGN * row_units + capacity, GROUP * row_units) * GROUP
    spill = pl.cdiv(slab_rows, LANES) * LANES
    steps = jnp.arange(SIDE, dtype=jnp.int32)

    matrix_id = data_index // PER_MATRIX
    holder = data_index < 2 * PER_MATRIX
    table_row = (matrix_id * n_feature + feature_index) * PER_MATRIX + data_index % PER_MATRIX
    my_entry = lax.dynamic_index_in_dim(
        shard_table, jnp.minimum(table_row, shard_table.shape[0] - 1), 0, keepdims=False
    )
    lead = (my_entry[0] - first_row * row_units) % (ALIGN * row_units)
    place = jnp.stack([lead, jnp.where(holder, my_entry[1], 0)])
    firsts = shard_table[:, 0].reshape(2, n_feature, PER_MATRIX)
    firsts = lax.dynamic_index_in_dim(firsts, feature_index, 1, keepdims=False).reshape(-1)
    offsets = (firsts // row_units - first_row) // ALIGN * ALIGN
    unpack_meta = jnp.concatenate([offsets, x[None]]).astype(jnp.int32)
    edge_block = 2 * ((z + steps) % SIDE)
    forward_meta = jnp.concatenate(
        [(y - z - steps) % SIDE, (x + 1)[None] % SIDE, edge_block + core, edge_block + 1 - core]
    )
    backward_meta = (y - z + steps) % SIDE
    swiglu_meta = jnp.stack([core, x]).astype(jnp.int32)

    shard = old_shards[0, 0]
    pack_chunks = functools.partial(
        pack, shard=shard, n_owner=n_data, row_units=row_units, slab_rows=slab_rows
    )
    groups = [[z * SIDE + x for x in range(SIDE)] for z in range(SIDE)]
    outgoing = list(pack_chunks(place, base=0, chunks=CHUNKS[:1]))
    rows = stacked_over_y(tokens)
    edge = from_first_x(features_ahead(tokens, spill))
    outgoing, rows, edge, place = lax.optimization_barrier((outgoing, rows, edge, place))
    incoming = [exchange(outgoing[0])]
    outgoing += list(pack_chunks(place, base=sum(CHUNKS[0]), chunks=CHUNKS[1:]))
    gathered = [rows] + [along_x(rows, s) for s in range(1, SIDE)]
    edges = lax.all_gather(edge, "dp", axis=0)
    sibling = [to_sibling(part) for part in gathered]
    outgoing, gathered, edges, unpack_meta, forward_meta, backward_meta, swiglu_meta = (
        lax.optimization_barrier(
            (outgoing, gathered, edges, unpack_meta, forward_meta, backward_meta, swiglu_meta)
        )
    )
    gathered = gathered + sibling
    for slabs in outgoing[1:]:
        incoming.append(exchange(after(slabs, incoming[-1])))

    weights, parts, grads, pieces = {}, {}, {}, {}
    latest = outgoing[1]
    for step in ORDER:
        index = int(step[1])
        chunk = CHUNKS[index]
        base = sum(sum(earlier) for earlier in CHUNKS[:index])
        if step[0] == "u":
            slabs = after(incoming[index], latest)
            columns = unpack(unpack_meta, slabs, block_rows + slab_rows, chunk)
            weights[index] = [columns[0]] + [along_x(columns[s], s) for s in range(1, SIDE)]
            if index == 0:
                source = after(cotangent, weights[0])
                upstream = lax.all_gather(
                    source, "fsdp", axis=0, tiled=True, axis_index_groups=groups
                )
            latest = columns[0]
        if step[0] == "f":
            own = [after(weights[index][0], latest)] + weights[index][1:]
            partial = forward(forward_meta, gathered, edges, own)
            parts[index] = [partial[0]] + [along_z(partial[s], s) for s in range(1, SIDE)]
            latest = partial[0]
        if step[0] == "s":
            own = [after(parts[index][0], latest)] + parts[index][1:]
            latest = swiglu_backward(swiglu_meta, own, upstream, base, chunk)
            below, above = along_z(latest, 1), along_z(latest, -1)
            if index + 1 < len(CHUNKS):
                opposite = [along_z(latest, 2)]
            else:
                half = latest.shape[0] // 2
                opposite = [along_z(below[:half], 1), along_z(above[half:], -1)]
            grads[index] = [latest, below, above] + opposite
        if step[0] == "b":
            own = [after(grads[index][0], latest, pieces)] + grads[index][1:]
            sums = backward(backward_meta, gathered, own)
            pieces[index] = [sums[0]] + [along_x(sums[s], -s) for s in range(1, SIDE)]
            latest = sums[0]
    finished = [piece for index in range(len(CHUNKS)) for piece in pieces[index]]
    return tuple(assemble(x[None], finished, hidden))


def solution(mesh):
    return jax.shard_map(
        on_device,
        mesh=mesh,
        in_specs=(P("dp", "fsdp", None, None), P(), P("dp", "fsdp"), P("fsdp", "dp")),
        out_specs=(P("fsdp", "dp"), P("fsdp", "dp")),
        check_vma=False,
    )
```
